32 devices in a mesh: section: 2 (over core), expert: 8 (over z, x), tensor: 2 (over y).
Axes of the slice: x: 2, y: 2, z: 4, core: 2. Of those that a mesh axis runs over, the one named last changes fastest.
Arguments:
- sent: bfloat16 [2, 256, 4096], P('section', ('expert', 'tensor')), may hold values from -20 to 20
- norm_gain: float32 [2, 4096], P('section'), may hold values from 0.1 to 1.9
- router: bfloat16 [2, 4096, 8], P('section'), may hold values from -0.09375 to 0.09375
- w_in: bfloat16 [2, 8, 4096, 2048], P('section', 'expert', None, 'tensor'), may hold values from -0.09375 to 0.09375
- w_out: bfloat16 [2, 8, 2048, 4096], P('section', 'expert', 'tensor'), may hold values from -0.125 to 0.125
- expert_ids: int32 [2, 256, 2], P('section', ('expert', 'tensor')), may hold values from 0 to 7, as said below
Outputs:
- handed: bfloat16 [2, 256, 4096], P('section', ('expert', 'tensor'))
The draws below stay inside these ranges and needn't reach their ends.
Inputs may be any that keep to these rules, and one draw needn't show every extreme that they name: `expert_ids`: each token names two different experts of the 8.
All inputs are finite; a program needn't handle non-finite values.
Results may differ from the reference program's by a relative error of at most 0.0054.
Values may be sent and summed in bfloat16 or wider, within the bound.
A program may use at most 64 MiB of HBM per device.

```python
import jax
import jax.numpy as jnp
from jax import lax

D = 4096
FF = 2048
TOK_DEV = 16
EXPERTS = 8
CAP = 5
TOKENS = 256
N_SECTION = 2
N_TENSOR = 2


def draw_sent(key, part):
    subkeys = jax.random.split(key, 3)
    values = jnp.clip(jax.random.normal(subkeys[0], (N_SECTION, TOKENS, D), jnp.float32), -4.0, 4.0)
    row_scale = jnp.exp(jax.random.uniform(subkeys[1], (N_SECTION, TOKENS, 1), jnp.float32, -0.8, 0.8))
    col_scale = jnp.exp(jax.random.uniform(subkeys[2], (N_SECTION, 1, D), jnp.float32, -0.8, 0.8))
    return (values * row_scale * col_scale).astype(jnp.bfloat16)


def draw_expert_ids(key, part):
    subkeys = jax.random.split(key, 5)
    grid_shape = (N_SECTION, TOKENS)
    lowest = jnp.minimum(jax.random.randint(subkeys[0], grid_shape, 0, EXPERTS), jax.random.randint(subkeys[1], grid_shape, 0, EXPERTS))
    lowest = jnp.minimum(lowest, jax.random.randint(subkeys[2], grid_shape, 0, EXPERTS))
    relabel = jax.random.permutation(subkeys[3], EXPERTS).astype(jnp.int32)
    first_pick = relabel[lowest]
    offset = jax.random.randint(subkeys[4], grid_shape, 1, EXPERTS)
    second_pick = (first_pick + offset) % EXPERTS
    return jnp.stack([first_pick, second_pick], axis=-1).astype(jnp.int32)


def levels(rng, dims, cuts, low, largest):
    factor_of = 1.0
    for dim, parts in cuts:
        steps = jax.random.uniform(jax.random.fold_in(jax.random.fold_in(rng, 6), dim), (parts,), jnp.float32, low / len(cuts), largest / len(cuts))
        factor_of = factor_of * jnp.repeat(jnp.exp(steps), dims[dim] // parts).reshape((-1,) + (1,) * (len(dims) - 1 - dim))
    return factor_of


def bell_draw(key, extent, deviation, most, shards=(), held_as=jnp.bfloat16):
    gain = levels(key, extent, shards, -0.22, 0.18) if shards else 1.0
    values = jax.random.normal(key, extent, jnp.float32) * deviation * gain
    return jnp.minimum(jnp.maximum(values, -most), most).astype(held_as)


def setup_inputs(seed: int = 0) -> dict:
    arg_keys = jax.random.split(jax.random.key(seed), 7)
    return {
        "sent": draw_sent(jax.random.fold_in(arg_keys[6], 71), 0),
        "norm_gain": jnp.clip(1.0 + 0.18 * jax.random.normal(arg_keys[1], (N_SECTION, D), jnp.float32), 0.1, 1.9),
        "router": bell_draw(arg_keys[2], (N_SECTION, D, EXPERTS), D ** -0.5, 0.09375, ((0, 2),)),
        "w_in": bell_draw(arg_keys[3], (N_SECTION, EXPERTS, D, FF), D ** -0.5, 0.09375, ((0, 2), (1, 8), (3, 2))),
        "w_out": bell_draw(arg_keys[4], (N_SECTION, EXPERTS, FF, D), FF ** -0.5, 0.125, ((0, 2), (1, 8), (2, 2))),
        "expert_ids": draw_expert_ids(jax.random.fold_in(arg_keys[6], 71), 0),
    }


def normalize(inputs, gain_row):
    widened = inputs.astype(jnp.float32)
    mean_sq = lax.optimization_barrier(jnp.mean(widened * widened, axis=-1, keepdims=True))
    return (widened * lax.rsqrt(mean_sq + 1e-05) * gain_row).astype(jnp.bfloat16)

def route(normed, router_mat, expert_pick, tok_block, capacity):
    logits = jnp.dot(normed, router_mat, preferred_element_type=jnp.float32)
    experts = router_mat.shape[1]
    labels = jnp.arange(experts, dtype=jnp.int32)
    pair_hot = (expert_pick[:, :, None] == labels[None, None, :]).astype(jnp.float32)
    picked = lax.optimization_barrier(jnp.sum(pair_hot * logits[:, None, :], axis=-1))
    squashed = jax.nn.sigmoid(picked)
    gate_vals = squashed / lax.optimization_barrier(jnp.sum(squashed, axis=-1, keepdims=True))
    blocks = expert_pick.shape[0] // tok_block
    pair_order = jnp.transpose(expert_pick.reshape(blocks, tok_block, 2), (0, 2, 1)).reshape(blocks, 2 * tok_block)
    one_hot = (pair_order[:, :, None] == labels[None, None, :]).astype(jnp.int32)
    before = (jnp.cumsum(one_hot, axis=1) - one_hot).astype(jnp.int32)
    pair_ranks = lax.optimization_barrier(jnp.sum(before * one_hot, axis=-1)).astype(jnp.int32)
    pair_ranks = jnp.transpose(pair_ranks.reshape(blocks, 2, tok_block), (0, 2, 1)).reshape(-1, 2)
    is_kept = pair_ranks < capacity
    return (gate_vals, pair_ranks, is_kept)

def layer(inputs, gain_row, router_mat, w_first, w_second, expert_pick):
    normed = normalize(inputs, gain_row)
    gate_vals, pair_ranks, is_kept = route(normed, router_mat, expert_pick, TOK_DEV, CAP)
    tok_total = inputs.shape[0]
    blocks = tok_total // TOK_DEV
    block_of = (jnp.arange(tok_total, dtype=jnp.int32) // TOK_DEV)[:, None]
    flat_slot = (expert_pick * (blocks * CAP) + block_of * CAP + pair_ranks).astype(jnp.int32)
    slot_total = EXPERTS * blocks * CAP
    target = jnp.where(is_kept, flat_slot, slot_total).reshape(-1)
    source_tok = jnp.broadcast_to(jnp.arange(tok_total, dtype=jnp.int32)[:, None], (tok_total, 2)).reshape(-1)
    owner_row = jnp.full((slot_total,), tok_total, jnp.int32).at[target].set(source_tok, mode='drop')
    padded = jnp.concatenate([normed, jnp.zeros((1, D), jnp.bfloat16)], axis=0)
    slot_rows = padded[owner_row].reshape(EXPERTS, blocks * CAP, D)
    group_width = FF // N_TENSOR

    def expert_ffn(operands):
        rows_in, first_mat, second_mat = operands
        hidden = jax.nn.gelu(jnp.dot(rows_in, first_mat, preferred_element_type=jnp.float32)).astype(jnp.bfloat16)
        summed = jnp.zeros((rows_in.shape[0], D), jnp.float32)
        for group_idx in range(N_TENSOR):
            lower = group_idx * group_width
            partial_value = jnp.dot(hidden[:, lower:lower + group_width], second_mat[lower:lower + group_width], preferred_element_type=jnp.float32).astype(jnp.bfloat16)
            summed = summed + partial_value.astype(jnp.float32)
        return summed.astype(jnp.bfloat16)
    expert_out = lax.map(expert_ffn, (slot_rows, w_first, w_second)).reshape(slot_total, D)
    picked = expert_out[jnp.where(is_kept, flat_slot, 0)].astype(jnp.float32)
    pair_weight = jnp.where(is_kept, gate_vals, 0.0)
    return (inputs.astype(jnp.float32) + lax.optimization_barrier(jnp.sum(pair_weight[:, :, None] * picked, axis=1))).astype(jnp.bfloat16)

def reference(sent, norm_gain, router, w_in, w_out, expert_ids):
    layer_outs = []
    for section_idx in range(N_SECTION):
        prior = (section_idx - 1) % N_SECTION
        layer_outs.append(layer(sent[prior], norm_gain[section_idx], router[section_idx], w_in[section_idx], w_out[section_idx], expert_ids[section_idx]))
    handed = [layer_outs[(section_idx - 1) % N_SECTION] for section_idx in range(N_SECTION)]
    return jnp.stack(handed)
```

```python
import functools

import jax
import jax.numpy as jnp
from jax import lax
from jax.experimental import pallas as pl
from jax.experimental.pallas import tpu as pltpu
from jax.sharding import PartitionSpec as P

MESH = pl.DeviceIdType.MESH
F32 = jnp.float32
BF16 = jnp.bfloat16
LANES = 128


def kernel(
    n_expert, n_tensor, cap, tok,
    x_ref, gain_slab, gain_row, router_t, ids_ref, w1_hbm, w2_hbm,
    out_ref,
    w1, w2, pad_ids, meta_send, meta_recv, aux_send, aux_recv, logit_pad,
    gathered, disp, got, flat, lhs, hid, partial, part_send, part_recv, ret_send, ret_recv, back,
    w_sem, meta_sem, aux_sem, disp_ss, disp_rs, fwd_ss, fwd_rs, part_ss, part_rs, ret_ss, ret_rs,
):
    core, e, t = lax.axis_index("section"), lax.axis_index("expert"), lax.axis_index("tensor")
    peer = 1 - core
    width = x_ref.shape[1]
    chunks = width // LANES
    half = chunks // 2
    slots = n_expert * cap
    mine = slots
    rows = n_tensor * slots
    ff = w1.shape[1]

    load1 = pltpu.make_async_copy(w1_hbm, w1, w_sem.at[0])
    load2 = pltpu.make_async_copy(w2_hbm, w2, w_sem.at[1])
    load1.start()
    load2.start()

    barrier = pltpu.get_barrier_semaphore()

    def greet(i, carry):
        pl.semaphore_signal(
            barrier, inc=1, device_id=(peer, lax.rem(e + i, n_expert), t), device_id_type=MESH
        )
        return carry

    lax.fori_loop(0, n_expert, greet, 0)
    for d in range(1, n_tensor):
        pl.semaphore_signal(
            barrier, inc=1, device_id=(core, e, lax.rem(t + d, n_tensor)), device_id_type=MESH
        )

    pad_ids[...] = jnp.full(pad_ids.shape, -1, jnp.int32)
    pad_ids[0:2, 0:tok] = ids_ref[...]
    label_rows = max(16, n_expert)
    labels = lax.broadcasted_iota(jnp.int32, (label_rows, LANES), 0)
    hot = [(labels == pad_ids[k:k + 1, :]) for k in range(2)]
    hot_f = [jnp.where(h, 1.0, 0.0).astype(F32) for h in hot]
    earlier = jnp.where(
        lax.broadcasted_iota(jnp.int32, (LANES, LANES), 0)
        < lax.broadcasted_iota(jnp.int32, (LANES, LANES), 1), 1.0, 0.0
    ).astype(BF16)
    before = [jnp.dot(h.astype(BF16), earlier, preferred_element_type=F32) for h in hot_f]
    before[1] = before[1] + jnp.sum(hot_f[0], axis=1, keepdims=True)
    meta_send[...] = pad_ids[...]
    for k in range(2):
        rank = jnp.sum(hot_f[k] * before[k], axis=0, keepdims=True).astype(jnp.int32)
        pick = pad_ids[k:k + 1, :]
        kept = jnp.logical_and(rank < cap, pick >= 0)
        meta_send[2 + k:3 + k, :] = jnp.where(kept, pick * cap + rank, -1)
    aux_send[0:n_expert, :] = router_t[...].astype(F32)
    aux_send[n_expert:n_expert + 8, :] = jnp.broadcast_to(gain_row[...], (8, width))

    pl.semaphore_wait(barrier, n_expert + n_tensor - 1)

    meta_copy = pltpu.make_async_remote_copy(
        meta_send, meta_recv, meta_sem.at[0], meta_sem.at[1], device_id=(peer, e, t), device_id_type=MESH
    )
    meta_copy.start()
    aux_copy = pltpu.make_async_remote_copy(
        aux_send, aux_recv, aux_sem.at[0], aux_sem.at[1], device_id=(peer, e, t), device_id_type=MESH
    )
    meta_copy.wait()
    aux_copy.start()

    slot_rows = back.shape[0] // half
    slot_labels = lax.broadcasted_iota(jnp.int32, (LANES, LANES), 0)
    place = [slot_labels == meta_recv[2 + k:3 + k, :] for k in range(2)]
    place_f = [jnp.where(m, 1.0, 0.0).astype(F32) for m in place]
    spread = (place_f[0] + place_f[1])[0:slot_rows, 0:tok].astype(BF16)
    rows_f = jnp.dot(spread, x_ref[...], preferred_element_type=F32)
    for c in range(chunks):
        gathered[pl.ds(c, slots, stride=chunks), :] = rows_f[0:slots, c * LANES:(c + 1) * LANES]
    disp[...] = gathered[...].reshape(disp.shape).astype(BF16)

    def disp_copy(i, sending):
        target = lax.rem(e + i, n_expert)
        return pltpu.make_async_remote_copy(
            disp.at[target], got.at[0, lax.rem(n_expert - i, n_expert) if sending else i],
            disp_ss.at[i], disp_rs.at[lax.rem(n_expert - i, n_expert) if sending else i],
            device_id=(peer, target, t), device_id_type=MESH,
        )

    def fwd_copy(d, i, sending):
        there = (n_tensor - d) if sending else d
        return pltpu.make_async_remote_copy(
            got.at[0, i], got.at[there, i], fwd_ss.at[d, i], fwd_rs.at[there, i],
            device_id=(core, e, lax.rem(t + d, n_tensor)), device_id_type=MESH,
        )

    def send_disp(i, carry):
        disp_copy(i, True).start()
        return carry

    lax.fori_loop(0, n_expert, send_disp, 0)

    def normalise(d, i):
        piece = got[d, i].astype(F32).reshape(cap, chunks, LANES)
        total = jnp.sum(jnp.sum(piece * piece, axis=1, keepdims=True), axis=2, keepdims=True)
        scale = lax.rsqrt(total * (1.0 / width) + 1e-05)
        normed = (piece * scale * gain_slab[...][None]).astype(BF16).astype(F32)
        start = pl.multiple_of((d * n_expert + i) * (cap * chunks), cap * chunks)
        flat[pl.ds(start, cap * chunks), :] = normed.reshape(cap * chunks, LANES)

    def take(i, carry):
        disp_copy(i, False).wait_recv()
        for d in range(1, n_tensor):
            fwd_copy(d, i, True).start()
        normalise(0, i)
        return carry

    lax.fori_loop(0, n_expert, take, 0)
    for d in range(1, n_tensor):
        def take_fwd(i, carry, d=d):
            fwd_copy(d, i, False).wait_recv()
            normalise(d, i)
            return carry

        lax.fori_loop(0, n_expert, take_fwd, 0)

    for c in range(chunks):
        lhs[:, c * LANES:(c + 1) * LANES] = flat[pl.ds(c, rows, stride=chunks), :].astype(BF16)

    tile = 256
    load1.wait()

    def first(n, carry):
        cols = pl.ds(pl.multiple_of(n * tile, tile), tile)
        value = jnp.dot(lhs[...], w1[:, cols], preferred_element_type=F32)
        hid[:, cols] = jax.nn.gelu(value).astype(BF16)
        return carry

    lax.fori_loop(0, ff // tile, first, 0)
    load2.wait()

    def part_copy(h, d, sending):
        there = (n_tensor - d) if sending else d
        return pltpu.make_async_remote_copy(
            part_send.at[h, d], part_recv.at[h, there], part_ss.at[h, d], part_rs.at[h, there],
            device_id=(core, e, lax.rem(t + d, n_tensor)), device_id_type=MESH,
        )

    def ret_copy(h, i, sending):
        target = lax.rem(e + i, n_expert)
        where = e if sending else target
        return pltpu.make_async_remote_copy(
            ret_send.at[h, i], ret_recv.at[h, where], ret_ss.at[h, i], ret_rs.at[h, where],
            device_id=(peer, target, t), device_id_type=MESH,
        )

    piece_rows = mine * half

    for h in range(2):
        def second(n, carry, h=h):
            cols = pl.ds(pl.multiple_of(h * half * LANES + n * tile, tile), tile)
            value = jnp.dot(hid[...], w2[:, cols], preferred_element_type=F32)
            for j in range(tile // LANES):
                partial[h, pl.ds(n * (tile // LANES) + j, rows, stride=half), :] = (
                    value[:, j * LANES:(j + 1) * LANES]
                )
            return carry

        lax.fori_loop(0, half * LANES // tile, second, 0)
        for d in range(1, n_tensor):
            part_send[h, d] = partial[h, d * piece_rows:(d + 1) * piece_rows, :].astype(BF16)
            part_copy(h, d, True).start()

    def reduce(h):
        total = partial[h, 0:piece_rows, :].astype(BF16).astype(F32)
        for d in range(1, n_tensor):
            part_copy(h, d, False).wait_recv()
            total = total + part_recv[h, d].astype(F32)
        ret_send[h] = total.astype(BF16).reshape(n_expert, cap * half, LANES)

        def send(i, carry):
            ret_copy(h, i, True).start()
            return carry

        lax.fori_loop(0, n_expert, send, 0)

    reduce(0)
    reduce(1)

    aux_copy.wait()
    x_f = x_ref[...].astype(F32)
    mean_sq = jnp.mean(x_f * x_f, axis=-1, keepdims=True)
    normed = (x_f * lax.rsqrt(mean_sq + 1e-05) * aux_recv[n_expert:n_expert + 1, :]).astype(BF16)
    logit_pad[...] = jnp.zeros(logit_pad.shape, F32)
    logit_pad[0:n_expert, 0:tok] = lax.dot_general(
        aux_recv[0:n_expert, :].astype(BF16), normed, (((1,), (1,)), ((), ())), preferred_element_type=F32
    )
    squashed = []
    for k in range(2):
        hit = labels == meta_recv[k:k + 1, :]
        squashed.append(
            jax.nn.sigmoid(jnp.sum(jnp.where(hit, logit_pad[...], 0.0), axis=0, keepdims=True))
        )
    both = squashed[0] + squashed[1]
    weights = place_f[0] * (squashed[0] / both) + place_f[1] * (squashed[1] / both)
    combine = jnp.transpose(weights)[0:tok, 0:slot_rows]
    high = combine.astype(BF16)
    rest = combine - high.astype(F32)
    mid = rest.astype(BF16)
    low = (rest - mid.astype(F32)).astype(BF16)
    if slot_rows > slots:
        back[slots * half:slot_rows * half, :] = jnp.zeros(((slot_rows - slots) * half, LANES), F32)

    for h in range(2):
        def arrive(i, carry, h=h):
            ret_copy(h, i, False).wait_recv()
            return carry

        lax.fori_loop(0, n_expert, arrive, 0)
        back[0:slots * half, :] = ret_recv[h].reshape(slots * half, LANES).astype(F32)
        table = jnp.concatenate(
            [back[pl.ds(c, slot_rows, stride=half), :].astype(BF16) for c in range(half)], axis=1
        )
        cols = slice(h * half * LANES, (h + 1) * half * LANES)
        added = jnp.dot(high, table, preferred_element_type=F32)
        added = added + jnp.dot(mid, table, preferred_element_type=F32)
        added = added + jnp.dot(low, table, preferred_element_type=F32)
        out_ref[:, cols] = (x_ref[:, cols].astype(F32) + added).astype(BF16)

    def drain(i, carry):
        disp_copy(i, True).wait_send()
        for d in range(1, n_tensor):
            fwd_copy(d, i, True).wait_send()
        for h in range(2):
            ret_copy(h, i, True).wait_send()
        return carry

    lax.fori_loop(0, n_expert, drain, 0)
    for h in range(2):
        for d in range(1, n_tensor):
            part_copy(h, d, True).wait_send()


def on_device(sent, norm_gain, router, w_in, w_out, expert_ids):
    tok, width = sent.shape[1], sent.shape[2]
    n_expert, n_tensor = lax.axis_size("expert"), lax.axis_size("tensor")
    top = expert_ids.shape[2]
    ff = w_in.shape[3]
    cap = max(2, (5 * top * tok + 4 * n_expert - 1) // (4 * n_expert))
    slots = n_expert * cap
    slot_rows = -(-slots // 16) * 16
    rows = n_tensor * slots
    chunks = width // LANES
    half = chunks // 2
    vmem = pl.BlockSpec(memory_space=pltpu.VMEM)
    hbm = pl.BlockSpec(memory_space=pl.ANY)
    dma = pltpu.SemaphoreType.DMA
    result = pl.pallas_call(
        functools.partial(kernel, n_expert, n_tensor, cap, tok),
        out_shape=jax.ShapeDtypeStruct((tok, width), BF16),
        in_specs=[vmem, vmem, vmem, vmem, vmem, hbm, hbm],
        out_specs=vmem,
        scratch_shapes=[
            pltpu.VMEM((width, ff), BF16),
            pltpu.VMEM((ff, width), BF16),
            pltpu.VMEM((8, LANES), jnp.int32),
            pltpu.VMEM((8, LANES), jnp.int32),
            pltpu.VMEM((8, LANES), jnp.int32),
            pltpu.VMEM((n_expert + 8, width), F32),
            pltpu.VMEM((n_expert + 8, width), F32),
            pltpu.VMEM((max(16, n_expert), LANES), F32),
            pltpu.VMEM((slots * chunks, LANES), F32),
            pltpu.VMEM((n_expert, cap * chunks, LANES), BF16),
            pltpu.VMEM((n_tensor, n_expert, cap * chunks, LANES), BF16),
            pltpu.VMEM((rows * chunks, LANES), F32),
            pltpu.VMEM((rows, width), BF16),
            pltpu.VMEM((rows, ff), BF16),
            pltpu.VMEM((2, rows * half, LANES), F32),
            pltpu.VMEM((2, n_tensor, slots * half, LANES), BF16),
            pltpu.VMEM((2, n_tensor, slots * half, LANES), BF16),
            pltpu.VMEM((2, n_expert, cap * half, LANES), BF16),
            pltpu.VMEM((2, n_expert, cap * half, LANES), BF16),
            pltpu.VMEM((slot_rows * half, LANES), F32),
            dma((2,)),
            dma((2,)),
            dma((2,)),
            dma((n_expert,)),
            dma((n_expert,)),
            dma((n_tensor, n_expert)),
            dma((n_tensor, n_expert)),
            dma((2, n_tensor)),
            dma((2, n_tensor)),
            dma((2, n_expert)),
            dma((2, n_expert)),
        ],
        compiler_params=pltpu.CompilerParams(
            collective_id=0, has_side_effects=True, vmem_limit_bytes=56 * 2**20
        ),
        name="expert_layer",
    )(
        sent[0],
        norm_gain.reshape(chunks, LANES),
        norm_gain,
        jnp.transpose(router[0]),
        jnp.transpose(expert_ids[0]),
        w_in[0, 0],
        w_out[0, 0],
    )
    return result[None]


def solution(mesh):
    return jax.shard_map(
        on_device,
        mesh=mesh,
        in_specs=(
            P("section", ("expert", "tensor"), None),
            P("section", None),
            P("section", None, None),
            P("section", "expert", None, "tensor"),
            P("section", "expert", "tensor", None),
            P("section", ("expert", "tensor"), None),
        ),
        out_specs=P("section", ("expert", "tensor"), None),
        check_vma=False,
    )
```

```python
import functools

import jax
import jax.numpy as jnp
from jax import lax
from jax.experimental import pallas as pl
from jax.experimental.pallas import tpu as pltpu
from jax.sharding import PartitionSpec as P

MESH = pl.DeviceIdType.MESH
F32 = jnp.float32
BF16 = jnp.bfloat16
LANES = 128


def flip(index, mask, count):
    total, bit = 0, 1
    while bit < count:
        total = total + lax.rem(index // bit + mask // bit, 2) * bit
        bit *= 2
    return total


def kernel(
    n_expert, n_tensor, cap, tok,
    x_ref, gain_slab, gain_row, router_t, ids_ref, w1_hbm, w2_hbm,
    out_ref,
    w1, w2, pad_ids, meta_send, meta_recv, aux_send, aux_recv, logit_pad,
    gathered, disp, got, flat, lhs, hid, partial, part_send, part_recv, ret_send, ret_recv, back,
    w_sem, meta_sem, aux_sem, disp_ss, disp_rs, fwd_ss, fwd_rs, part_ss, part_rs, ret_ss, ret_rs,
):
    core, e, t = lax.axis_index("section"), lax.axis_index("expert"), lax.axis_index("tensor")
    peer = 1 - core
    width = x_ref.shape[1]
    chunks = width // LANES
    half = chunks // 2
    slots = n_expert * cap
    rows = n_tensor * slots
    ff = w1.shape[1]

    load1 = pltpu.make_async_copy(w1_hbm, w1, w_sem.at[0])
    load2 = pltpu.make_async_copy(w2_hbm, w2, w_sem.at[1])
    load1.start()
    load2.start()

    barrier = pltpu.get_barrier_semaphore()

    def greet(i, carry):
        pl.semaphore_signal(
            barrier, inc=1, device_id=(peer, lax.rem(e + i, n_expert), t), device_id_type=MESH
        )
        return carry

    lax.fori_loop(0, n_expert, greet, 0)
    for d in range(1, n_tensor):
        pl.semaphore_signal(
            barrier, inc=1, device_id=(core, e, lax.rem(t + d, n_tensor)), device_id_type=MESH
        )

    pad_ids[...] = jnp.full(pad_ids.shape, -1, jnp.int32)
    pad_ids[0:2, 0:tok] = ids_ref[...]
    label_rows = max(16, n_expert)
    labels = lax.broadcasted_iota(jnp.int32, (label_rows, LANES), 0)
    hot = [(labels == pad_ids[k:k + 1, :]) for k in range(2)]
    hot_f = [jnp.where(h, 1.0, 0.0).astype(F32) for h in hot]
    earlier = jnp.where(
        lax.broadcasted_iota(jnp.int32, (LANES, LANES), 0)
        < lax.broadcasted_iota(jnp.int32, (LANES, LANES), 1), 1.0, 0.0
    ).astype(BF16)
    before = [jnp.dot(h.astype(BF16), earlier, preferred_element_type=F32) for h in hot_f]
    before[1] = before[1] + jnp.sum(hot_f[0], axis=1, keepdims=True)
    meta_send[...] = pad_ids[...]
    for k in range(2):
        rank = jnp.sum(hot_f[k] * before[k], axis=0, keepdims=True).astype(jnp.int32)
        pick = pad_ids[k:k + 1, :]
        kept = jnp.logical_and(rank < cap, pick >= 0)
        meta_send[2 + k:3 + k, :] = jnp.where(kept, pick * cap + rank, -1)
    aux_send[0:n_expert, :] = router_t[...].astype(F32)
    aux_send[n_expert:n_expert + 8, :] = jnp.broadcast_to(gain_row[...], (8, width))

    pl.semaphore_wait(barrier, n_expert + n_tensor - 1)

    meta_copy = pltpu.make_async_remote_copy(
        meta_send, meta_recv, meta_sem.at[0], meta_sem.at[1], device_id=(peer, e, t), device_id_type=MESH
    )
    meta_copy.start()
    aux_copy = pltpu.make_async_remote_copy(
        aux_send, aux_recv, aux_sem.at[0], aux_sem.at[1], device_id=(peer, e, t), device_id_type=MESH
    )
    meta_copy.wait()
    aux_copy.start()

    slot_rows = back.shape[0] // half
    slot_labels = lax.broadcasted_iota(jnp.int32, (LANES, LANES), 0)
    place = [slot_labels == meta_recv[2 + k:3 + k, :] for k in range(2)]
    place_f = [jnp.where(m, 1.0, 0.0).astype(F32) for m in place]
    spread = (place_f[0] + place_f[1])[0:slot_rows, 0:tok].astype(BF16)
    rows_f = jnp.dot(spread, x_ref[...], preferred_element_type=F32)
    for c in range(chunks):
        gathered[pl.ds(c, slots, stride=chunks), :] = rows_f[0:slots, c * LANES:(c + 1) * LANES]
    disp[...] = gathered[...].reshape(disp.shape).astype(BF16)

    def disp_copy(i):
        target = flip(e, i, n_expert)
        return pltpu.make_async_remote_copy(
            disp.at[target], got.at[0, i], disp_ss.at[i], disp_rs.at[i],
            device_id=(peer, target, t), device_id_type=MESH,
        )

    def fwd_copy(d, i, sending):
        there = (n_tensor - d) if sending else d
        return pltpu.make_async_remote_copy(
            got.at[0, i], got.at[there, i], fwd_ss.at[d, i], fwd_rs.at[there, i],
            device_id=(core, e, lax.rem(t + d, n_tensor)), device_id_type=MESH,
        )

    def send_disp(i, carry):
        disp_copy(i).start()
        return carry

    lax.fori_loop(0, n_expert, send_disp, 0)

    def normalise(d, i):
        piece = got[d, i].astype(F32).reshape(cap, chunks, LANES)
        total = jnp.sum(jnp.sum(piece * piece, axis=1, keepdims=True), axis=2, keepdims=True)
        scale = lax.rsqrt(total * (1.0 / width) + 1e-05)
        normed = (piece * scale * gain_slab[...][None]).astype(BF16).astype(F32)
        start = pl.multiple_of((d * n_expert + i) * (cap * chunks), cap * chunks)
        flat[pl.ds(start, cap * chunks), :] = normed.reshape(cap * chunks, LANES)

    def take(i, carry):
        disp_copy(i).wait_recv()
        for d in range(1, n_tensor):
            fwd_copy(d, i, True).start()
        normalise(0, i)
        return carry

    lax.fori_loop(0, n_expert, take, 0)
    for d in range(1, n_tensor):
        def take_fwd(i, carry, d=d):
            fwd_copy(d, i, False).wait_recv()
            normalise(d, i)
            return carry

        lax.fori_loop(0, n_expert, take_fwd, 0)

    for c in range(chunks):
        lhs[:, c * LANES:(c + 1) * LANES] = flat[pl.ds(c, rows, stride=chunks), :].astype(BF16)

    tile = 256
    load1.wait()

    def first(n, carry):
        cols = pl.ds(pl.multiple_of(n * tile, tile), tile)
        value = jnp.dot(lhs[...], w1[:, cols], preferred_element_type=F32)
        hid[:, cols] = jax.nn.gelu(value).astype(BF16)
        return carry

    lax.fori_loop(0, ff // tile, first, 0)
    load2.wait()

    def part_copy(h, d, i, sending):
        there = (n_tensor - d) if sending else d
        return pltpu.make_async_remote_copy(
            part_send.at[h, d, i], part_recv.at[h, there, i], part_ss.at[h, d, i], part_rs.at[h, there, i],
            device_id=(core, e, lax.rem(t + d, n_tensor)), device_id_type=MESH,
        )

    def ret_copy(h, i, sending):
        target = flip(e, i, n_expert)
        where = e if sending else target
        return pltpu.make_async_remote_copy(
            ret_send.at[h, i], ret_recv.at[h, where], ret_ss.at[h, i], ret_rs.at[h, where],
            device_id=(peer, target, t), device_id_type=MESH,
        )

    piece_rows = cap * half

    for h in range(2):
        def second(n, carry, h=h):
            cols = pl.ds(pl.multiple_of(h * half * LANES + n * tile, tile), tile)
            value = jnp.dot(hid[...], w2[:, cols], preferred_element_type=F32)
            for j in range(tile // LANES):
                partial[h, pl.ds(n * (tile // LANES) + j, rows, stride=half), :] = (
                    value[:, j * LANES:(j + 1) * LANES]
                )
            return carry

        lax.fori_loop(0, half * LANES // tile, second, 0)
        for d in range(1, n_tensor):
            def send_part(k, carry, h=h, d=d):
                i = n_expert - 1 - k
                start = pl.multiple_of((d * n_expert + i) * piece_rows, piece_rows)
                part_send[h, d, i] = partial[h, pl.ds(start, piece_rows), :].astype(BF16)
                part_copy(h, d, i, True).start()
                return carry

            lax.fori_loop(0, n_expert, send_part, 0)

    def reduce(h):
        def one(k, carry):
            i = n_expert - 1 - k
            start = pl.multiple_of(i * piece_rows, piece_rows)
            total = partial[h, pl.ds(start, piece_rows), :].astype(BF16).astype(F32)
            for d in range(1, n_tensor):
                part_copy(h, d, i, False).wait_recv()
                total = total + part_recv[h, d, i].astype(F32)
            ret_send[h, i] = total.astype(BF16)
            ret_copy(h, i, True).start()
            return carry

        lax.fori_loop(0, n_expert, one, 0)

    reduce(0)
    reduce(1)

    aux_copy.wait()
    x_f = x_ref[...].astype(F32)
    mean_sq = jnp.mean(x_f * x_f, axis=-1, keepdims=True)
    normed = (x_f * lax.rsqrt(mean_sq + 1e-05) * aux_recv[n_expert:n_expert + 1, :]).astype(BF16)
    logit_pad[...] = jnp.zeros(logit_pad.shape, F32)
    logit_pad[0:n_expert, 0:tok] = lax.dot_general(
        aux_recv[0:n_expert, :].astype(BF16), normed, (((1,), (1,)), ((), ())), preferred_element_type=F32
    )
    squashed = []
    for k in range(2):
        hit = labels == meta_recv[k:k + 1, :]
        squashed.append(
            jax.nn.sigmoid(jnp.sum(jnp.where(hit, logit_pad[...], 0.0), axis=0, keepdims=True))
        )
    both = squashed[0] + squashed[1]
    weights = place_f[0] * (squashed[0] / both) + place_f[1] * (squashed[1] / both)
    combine = jnp.transpose(weights)[0:tok, 0:slot_rows]
    high = combine.astype(BF16)
    rest = combine - high.astype(F32)
    mid = rest.astype(BF16)
    low = (rest - mid.astype(F32)).astype(BF16)
    if slot_rows > slots:
        back[slots * half:slot_rows * half, :] = jnp.zeros(((slot_rows - slots) * half, LANES), F32)

    for h in range(2):
        def arrive(i, carry, h=h):
            ret_copy(h, i, False).wait_recv()
            return carry

        lax.fori_loop(0, n_expert, arrive, 0)
        back[0:slots * half, :] = ret_recv[h].reshape(slots * half, LANES).astype(F32)
        table = jnp.concatenate(
            [back[pl.ds(c, slot_rows, stride=half), :].astype(BF16) for c in range(half)], axis=1
        )
        cols = slice(h * half * LANES, (h + 1) * half * LANES)
        added = jnp.dot(high, table, preferred_element_type=F32)
        added = added + jnp.dot(mid, table, preferred_element_type=F32)
        added = added + jnp.dot(low, table, preferred_element_type=F32)
        out_ref[:, cols] = (x_ref[:, cols].astype(F32) + added).astype(BF16)

    def drain(i, carry):
        disp_copy(i).wait_send()
        for d in range(1, n_tensor):
            fwd_copy(d, i, True).wait_send()
        for h in range(2):
            ret_copy(h, i, True).wait_send()
            for d in range(1, n_tensor):
                part_copy(h, d, i, True).wait_send()
        return carry

    lax.fori_loop(0, n_expert, drain, 0)


def on_device(sent, norm_gain, router, w_in, w_out, expert_ids):
    tok, width = sent.shape[1], sent.shape[2]
    n_expert, n_tensor = lax.axis_size("expert"), lax.axis_size("tensor")
    top = expert_ids.shape[2]
    ff = w_in.shape[3]
    cap = max(2, (5 * top * tok + 4 * n_expert - 1) // (4 * n_expert))
    slots = n_expert * cap
    slot_rows = -(-slots // 16) * 16
    rows = n_tensor * slots
    chunks = width // LANES
    half = chunks // 2
    vmem = pl.BlockSpec(memory_space=pltpu.VMEM)
    hbm = pl.BlockSpec(memory_space=pl.ANY)
    dma = pltpu.SemaphoreType.DMA
    result = pl.pallas_call(
        functools.partial(kernel, n_expert, n_tensor, cap, tok),
        out_shape=jax.ShapeDtypeStruct((tok, width), BF16),
        in_specs=[vmem, vmem, vmem, vmem, vmem, hbm, hbm],
        out_specs=vmem,
        scratch_shapes=[
            pltpu.VMEM((width, ff), BF16),
            pltpu.VMEM((ff, width), BF16),
            pltpu.VMEM((8, LANES), jnp.int32),
            pltpu.VMEM((8, LANES), jnp.int32),
            pltpu.VMEM((8, LANES), jnp.int32),
            pltpu.VMEM((n_expert + 8, width), F32),
            pltpu.VMEM((n_expert + 8, width), F32),
            pltpu.VMEM((max(16, n_expert), LANES), F32),
            pltpu.VMEM((slots * chunks, LANES), F32),
            pltpu.VMEM((n_expert, cap * chunks, LANES), BF16),
            pltpu.VMEM((n_tensor, n_expert, cap * chunks, LANES), BF16),
            pltpu.VMEM((rows * chunks, LANES), F32),
            pltpu.VMEM((rows, width), BF16),
            pltpu.VMEM((rows, ff), BF16),
            pltpu.VMEM((2, rows * half, LANES), F32),
            pltpu.VMEM((2, n_tensor, n_expert, cap * half, LANES), BF16),
            pltpu.VMEM((2, n_tensor, n_expert, cap * half, LANES), BF16),
            pltpu.VMEM((2, n_expert, cap * half, LANES), BF16),
            pltpu.VMEM((2, n_expert, cap * half, LANES), BF16),
            pltpu.VMEM((slot_rows * half, LANES), F32),
            dma((2,)),
            dma((2,)),
            dma((2,)),
            dma((n_expert,)),
            dma((n_expert,)),
            dma((n_tensor, n_expert)),
            dma((n_tensor, n_expert)),
            dma((2, n_tensor, n_expert)),
            dma((2, n_tensor, n_expert)),
            dma((2, n_expert)),
            dma((2, n_expert)),
        ],
        compiler_params=pltpu.CompilerParams(
            collective_id=0, has_side_effects=True, vmem_limit_bytes=56 * 2**20
        ),
        name="expert_layer",
    )(
        sent[0],
        norm_gain.reshape(chunks, LANES),
        norm_gain,
        jnp.transpose(router[0]),
        jnp.transpose(expert_ids[0]),
        w_in[0, 0],
        w_out[0, 0],
    )
    return result[None]


def solution(mesh):
    return jax.shard_map(
        on_device,
        mesh=mesh,
        in_specs=(
            P("section", ("expert", "tensor"), None),
            P("section", None),
            P("section", None, None),
            P("section", "expert", None, "tensor"),
            P("section", "expert", "tensor", None),
            P("section", ("expert", "tensor"), None),
        ),
        out_specs=P("section", ("expert", "tensor"), None),
        check_vma=False,
    )
```

```python
import functools

import jax
import jax.numpy as jnp
from jax import lax
from jax.experimental import pallas as pl
from jax.experimental.pallas import tpu as pltpu
from jax.sharding import PartitionSpec as P

MESH = pl.DeviceIdType.MESH
F32 = jnp.float32
BF16 = jnp.bfloat16
LANES = 128


def flip(index, mask, count):
    total, bit = 0, 1
    while bit < count:
        total = total + lax.rem(index // bit + mask // bit, 2) * bit
        bit *= 2
    return total


def kernel(
    n_expert, n_tensor, cap, tok,
    x_hbm, slab_hbm, row_hbm, router_hbm, ids_ref, w1_hbm, w2_hbm,
    out_hbm,
    x_ref, gain_slab, gain_row, router_t, out_ref, w1, w2, pad_ids, meta_send, meta_recv, aux_send, aux_recv, logit_pad,
    gathered, disp, got, flat, lhs, hid, partial, part_send, part_recv, ret_send, ret_recv, back,
    in_sem, out_sem, w_sem, meta_sem, aux_sem, disp_ss, disp_rs, fwd_ss, fwd_rs, part_ss, part_rs, ret_ss, ret_rs,
):
    core, e, t = lax.axis_index("section"), lax.axis_index("expert"), lax.axis_index("tensor")
    peer = 1 - core
    width = x_ref.shape[1]
    chunks = width // LANES
    half = chunks // 2
    slots = n_expert * cap
    rows = n_tensor * slots
    ff = w1.shape[1]

    barrier = pltpu.get_barrier_semaphore()

    def greet(i, carry):
        pl.semaphore_signal(
            barrier, inc=1, device_id=(peer, lax.rem(e + i, n_expert), t), device_id_type=MESH
        )
        return carry

    lax.fori_loop(0, n_expert, greet, 0)
    for d in range(1, n_tensor):
        pl.semaphore_signal(
            barrier, inc=1, device_id=(core, e, lax.rem(t + d, n_tensor)), device_id_type=MESH
        )

    small = [
        pltpu.make_async_copy(src, dst, in_sem.at[n])
        for n, (src, dst) in enumerate(
            [(router_hbm, router_t), (row_hbm, gain_row), (x_hbm, x_ref), (slab_hbm, gain_slab)]
        )
    ]
    for copy in small:
        copy.start()
    load1 = pltpu.make_async_copy(w1_hbm, w1, w_sem.at[0])
    load2 = pltpu.make_async_copy(w2_hbm, w2, w_sem.at[1])
    load1.start()
    load2.start()

    pad_ids[...] = jnp.full(pad_ids.shape, -1, jnp.int32)
    pad_ids[0:2, 0:tok] = ids_ref[...]
    label_rows = max(16, n_expert)
    labels = lax.broadcasted_iota(jnp.int32, (label_rows, LANES), 0)
    hot = [(labels == pad_ids[k:k + 1, :]) for k in range(2)]
    hot_f = [jnp.where(h, 1.0, 0.0).astype(F32) for h in hot]
    earlier = jnp.where(
        lax.broadcasted_iota(jnp.int32, (LANES, LANES), 0)
        < lax.broadcasted_iota(jnp.int32, (LANES, LANES), 1), 1.0, 0.0
    ).astype(BF16)
    before = [jnp.dot(h.astype(BF16), earlier, preferred_element_type=F32) for h in hot_f]
    before[1] = before[1] + jnp.sum(hot_f[0], axis=1, keepdims=True)
    meta_send[...] = pad_ids[...]
    for k in range(2):
        rank = jnp.sum(hot_f[k] * before[k], axis=0, keepdims=True).astype(jnp.int32)
        pick = pad_ids[k:k + 1, :]
        kept = jnp.logical_and(rank < cap, pick >= 0)
        meta_send[2 + k:3 + k, :] = jnp.where(kept, pick * cap + rank, -1)
    small[0].wait()
    small[1].wait()
    aux_send[0:n_expert, :] = router_t[...].astype(F32)
    aux_send[n_expert:n_expert + 8, :] = jnp.broadcast_to(gain_row[...], (8, width))

    small[2].wait()
    small[3].wait()
    pl.semaphore_wait(barrier, n_expert + n_tensor - 1)

    meta_copy = pltpu.make_async_remote_copy(
        meta_send, meta_recv, meta_sem.at[0], meta_sem.at[1], device_id=(peer, e, t), device_id_type=MESH
    )
    meta_copy.start()
    aux_copy = pltpu.make_async_remote_copy(
        aux_send, aux_recv, aux_sem.at[0], aux_sem.at[1], device_id=(peer, e, t), device_id_type=MESH
    )
    meta_copy.wait()
    aux_copy.start()

    slot_rows = back.shape[0] // half
    slot_labels = lax.broadcasted_iota(jnp.int32, (LANES, LANES), 0)
    place = [slot_labels == meta_recv[2 + k:3 + k, :] for k in range(2)]
    place_f = [jnp.where(m, 1.0, 0.0).astype(F32) for m in place]
    spread = (place_f[0] + place_f[1])[0:slot_rows, 0:tok].astype(BF16)
    rows_f = jnp.dot(spread, x_ref[...], preferred_element_type=F32)
    for c in range(chunks):
        gathered[pl.ds(c, slots, stride=chunks), :] = rows_f[0:slots, c * LANES:(c + 1) * LANES]
    disp[...] = gathered[...].reshape(disp.shape).astype(BF16)

    def disp_copy(i):
        target = flip(e, i, n_expert)
        return pltpu.make_async_remote_copy(
            disp.at[target], got.at[0, i], disp_ss.at[i], disp_rs.at[i],
            device_id=(peer, target, t), device_id_type=MESH,
        )

    def fwd_copy(d, i, sending):
        there = (n_tensor - d) if sending else d
        return pltpu.make_async_remote_copy(
            got.at[0, i], got.at[there, i], fwd_ss.at[d, i], fwd_rs.at[there, i],
            device_id=(core, e, lax.rem(t + d, n_tensor)), device_id_type=MESH,
        )

    def send_disp(i, carry):
        disp_copy(i).start()
        return carry

    lax.fori_loop(0, n_expert, send_disp, 0)

    def normalise(d, i):
        piece = got[d, i].astype(F32).reshape(cap, chunks, LANES)
        total = jnp.sum(jnp.sum(piece * piece, axis=1, keepdims=True), axis=2, keepdims=True)
        scale = lax.rsqrt(total * (1.0 / width) + 1e-05)
        normed = (piece * scale * gain_slab[...][None]).astype(BF16).astype(F32)
        start = pl.multiple_of((d * n_expert + i) * (cap * chunks), cap * chunks)
        flat[pl.ds(start, cap * chunks), :] = normed.reshape(cap * chunks, LANES)

    def take(i, carry):
        disp_copy(i).wait_recv()
        for d in range(1, n_tensor):
            fwd_copy(d, i, True).start()
        normalise(0, i)
        return carry

    lax.fori_loop(0, n_expert, take, 0)
    for d in range(1, n_tensor):
        def take_fwd(i, carry, d=d):
            fwd_copy(d, i, False).wait_recv()
            normalise(d, i)
            return carry

        lax.fori_loop(0, n_expert, take_fwd, 0)

    for c in range(chunks):
        lhs[:, c * LANES:(c + 1) * LANES] = flat[pl.ds(c, rows, stride=chunks), :].astype(BF16)

    tile = 256
    load1.wait()

    def first(n, carry):
        cols = pl.ds(pl.multiple_of(n * tile, tile), tile)
        value = jnp.dot(lhs[...], w1[:, cols], preferred_element_type=F32)
        hid[:, cols] = jax.nn.gelu(value).astype(BF16)
        return carry

    lax.fori_loop(0, ff // tile, first, 0)
    load2.wait()

    def part_copy(h, d, i, sending):
        there = (n_tensor - d) if sending else d
        return pltpu.make_async_remote_copy(
            part_send.at[h, d, i], part_recv.at[h, there, i], part_ss.at[h, d, i], part_rs.at[h, there, i],
            device_id=(core, e, lax.rem(t + d, n_tensor)), device_id_type=MESH,
        )

    def ret_copy(h, i, sending):
        target = flip(e, i, n_expert)
        where = e if sending else target
        return pltpu.make_async_remote_copy(
            ret_send.at[h, i], ret_recv.at[h, where], ret_ss.at[h, i], ret_rs.at[h, where],
            device_id=(peer, target, t), device_id_type=MESH,
        )

    piece_rows = cap * half

    for h in range(2):
        def second(n, carry, h=h):
            cols = pl.ds(pl.multiple_of(h * half * LANES + n * tile, tile), tile)
            value = jnp.dot(hid[...], w2[:, cols], preferred_element_type=F32)
            for j in range(tile // LANES):
                partial[h, pl.ds(n * (tile // LANES) + j, rows, stride=half), :] = (
                    value[:, j * LANES:(j + 1) * LANES]
                )
            return carry

        lax.fori_loop(0, half * LANES // tile, second, 0)
        for d in range(1, n_tensor):
            def send_part(k, carry, h=h, d=d):
                i = n_expert - 1 - k
                start = pl.multiple_of((d * n_expert + i) * piece_rows, piece_rows)
                part_send[h, d, i] = partial[h, pl.ds(start, piece_rows), :].astype(BF16)
                part_copy(h, d, i, True).start()
                return carry

            lax.fori_loop(0, n_expert, send_part, 0)

    def reduce(h):
        def one(k, carry):
            i = n_expert - 1 - k
            start = pl.multiple_of(i * piece_rows, piece_rows)
            total = partial[h, pl.ds(start, piece_rows), :].astype(BF16).astype(F32)
            for d in range(1, n_tensor):
                part_copy(h, d, i, False).wait_recv()
                total = total + part_recv[h, d, i].astype(F32)
            ret_send[h, i] = total.astype(BF16)
            ret_copy(h, i, True).start()
            return carry

        lax.fori_loop(0, n_expert, one, 0)

    reduce(0)
    reduce(1)

    aux_copy.wait()
    x_f = x_ref[...].astype(F32)
    mean_sq = jnp.mean(x_f * x_f, axis=-1, keepdims=True)
    normed = (x_f * lax.rsqrt(mean_sq + 1e-05) * aux_recv[n_expert:n_expert + 1, :]).astype(BF16)
    logit_pad[...] = jnp.zeros(logit_pad.shape, F32)
    logit_pad[0:n_expert, 0:tok] = lax.dot_general(
        aux_recv[0:n_expert, :].astype(BF16), normed, (((1,), (1,)), ((), ())), preferred_element_type=F32
    )
    squashed = []
    for k in range(2):
        hit = labels == meta_recv[k:k + 1, :]
        squashed.append(
            jax.nn.sigmoid(jnp.sum(jnp.where(hit, logit_pad[...], 0.0), axis=0, keepdims=True))
        )
    both = squashed[0] + squashed[1]
    weights = place_f[0] * (squashed[0] / both) + place_f[1] * (squashed[1] / both)
    combine = jnp.transpose(weights)[0:tok, 0:slot_rows]
    high = combine.astype(BF16)
    rest = combine - high.astype(F32)
    mid = rest.astype(BF16)
    low = (rest - mid.astype(F32)).astype(BF16)
    if slot_rows > slots:
        back[slots * half:slot_rows * half, :] = jnp.zeros(((slot_rows - slots) * half, LANES), F32)

    stores = []
    for h in range(2):
        def arrive(i, carry, h=h):
            ret_copy(h, i, False).wait_recv()
            return carry

        lax.fori_loop(0, n_expert, arrive, 0)
        back[0:slots * half, :] = ret_recv[h].reshape(slots * half, LANES).astype(F32)
        table = jnp.concatenate(
            [back[pl.ds(c, slot_rows, stride=half), :].astype(BF16) for c in range(half)], axis=1
        )
        cols = slice(h * half * LANES, (h + 1) * half * LANES)
        added = jnp.dot(high, table, preferred_element_type=F32)
        added = added + jnp.dot(mid, table, preferred_element_type=F32)
        added = added + jnp.dot(low, table, preferred_element_type=F32)
        out_ref[h] = (x_ref[:, cols].astype(F32) + added).astype(BF16)
        store = pltpu.make_async_copy(out_ref.at[h], out_hbm.at[:, cols], out_sem.at[h])
        store.start()
        stores.append(store)

    def drain(i, carry):
        disp_copy(i).wait_send()
        for d in range(1, n_tensor):
            fwd_copy(d, i, True).wait_send()
        for h in range(2):
            ret_copy(h, i, True).wait_send()
            for d in range(1, n_tensor):
                part_copy(h, d, i, True).wait_send()
        return carry

    lax.fori_loop(0, n_expert, drain, 0)
    for store in stores:
        store.wait()


def on_device(sent, norm_gain, router, w_in, w_out, expert_ids):
    tok, width = sent.shape[1], sent.shape[2]
    n_expert, n_tensor = lax.axis_size("expert"), lax.axis_size("tensor")
    top = expert_ids.shape[2]
    ff = w_in.shape[3]
    cap = max(2, (5 * top * tok + 4 * n_expert - 1) // (4 * n_expert))
    slots = n_expert * cap
    slot_rows = -(-slots // 16) * 16
    rows = n_tensor * slots
    chunks = width // LANES
    half = chunks // 2
    vmem = pl.BlockSpec(memory_space=pltpu.VMEM)
    hbm = pl.BlockSpec(memory_space=pl.ANY)
    dma = pltpu.SemaphoreType.DMA
    result = pl.pallas_call(
        functools.partial(kernel, n_expert, n_tensor, cap, tok),
        out_shape=jax.ShapeDtypeStruct((tok, width), BF16),
        in_specs=[hbm, hbm, hbm, hbm, vmem, hbm, hbm],
        out_specs=hbm,
        scratch_shapes=[
            pltpu.VMEM((tok, width), BF16),
            pltpu.VMEM((chunks, LANES), F32),
            pltpu.VMEM((1, width), F32),
            pltpu.VMEM((n_expert, width), BF16),
            pltpu.VMEM((2, tok, width // 2), BF16),
            pltpu.VMEM((width, ff), BF16),
            pltpu.VMEM((ff, width), BF16),
            pltpu.VMEM((8, LANES), jnp.int32),
            pltpu.VMEM((8, LANES), jnp.int32),
            pltpu.VMEM((8, LANES), jnp.int32),
            pltpu.VMEM((n_expert + 8, width), F32),
            pltpu.VMEM((n_expert + 8, width), F32),
            pltpu.VMEM((max(16, n_expert), LANES), F32),
            pltpu.VMEM((slots * chunks, LANES), F32),
            pltpu.VMEM((n_expert, cap * chunks, LANES), BF16),
            pltpu.VMEM((n_tensor, n_expert, cap * chunks, LANES), BF16),
            pltpu.VMEM((rows * chunks, LANES), F32),
            pltpu.VMEM((rows, width), BF16),
            pltpu.VMEM((rows, ff), BF16),
            pltpu.VMEM((2, rows * half, LANES), F32),
            pltpu.VMEM((2, n_tensor, n_expert, cap * half, LANES), BF16),
            pltpu.VMEM((2, n_tensor, n_expert, cap * half, LANES), BF16),
            pltpu.VMEM((2, n_expert, cap * half, LANES), BF16),
            pltpu.VMEM((2, n_expert, cap * half, LANES), BF16),
            pltpu.VMEM((slot_rows * half, LANES), F32),
            dma((4,)),
            dma((2,)),
            dma((2,)),
            dma((2,)),
            dma((2,)),
            dma((n_expert,)),
            dma((n_expert,)),
            dma((n_tensor, n_expert)),
            dma((n_tensor, n_expert)),
            dma((2, n_tensor, n_expert)),
            dma((2, n_tensor, n_expert)),
            dma((2, n_expert)),
            dma((2, n_expert)),
        ],
        compiler_params=pltpu.CompilerParams(
            collective_id=0, has_side_effects=True, vmem_limit_bytes=56 * 2**20
        ),
        name="expert_layer",
    )(
        sent[0],
        norm_gain.reshape(chunks, LANES),
        norm_gain,
        jnp.transpose(router[0]),
        jnp.transpose(expert_ids[0]),
        w_in[0, 0],
        w_out[0, 0],
    )
    return result[None]


def solution(mesh):
    return jax.shard_map(
        on_device,
        mesh=mesh,
        in_specs=(
            P("section", ("expert", "tensor"), None),
            P("section", None),
            P("section", None, None),
            P("section", "expert", None, "tensor"),
            P("section", "expert", "tensor", None),
            P("section", ("expert", "tensor"), None),
        ),
        out_specs=P("section", ("expert", "tensor"), None),
        check_vma=False,
    )
```

```python
import functools

import jax
import jax.numpy as jnp
from jax import lax
from jax.experimental import pallas as pl
from jax.experimental.pallas import tpu as pltpu
from jax.sharding import PartitionSpec as P

MESH = pl.DeviceIdType.MESH
F32 = jnp.float32
BF16 = jnp.bfloat16
LANES = 128


def flip(index, mask, count):
    total, bit = 0, 1
    while bit < count:
        total = total + lax.rem(index // bit + mask // bit, 2) * bit
        bit *= 2
    return total


def kernel(
    n_expert, n_tensor, cap, tok,
    x_ref, gain_slab, gain_row, router_t, ids_ref, w1_hbm, w2_hbm,
    out_ref,
    w1, w2, pad_ids, meta_send, meta_recv, aux_send, aux_recv, logit_pad,
    gathered, disp, got, flat, lhs, hid, partial, part_send, part_recv, ret_send, ret_recv, back,
    w_sem, meta_sem, aux_sem, disp_ss, disp_rs, fwd_ss, fwd_rs, part_ss, part_rs, ret_ss, ret_rs,
):
    core, e, t = lax.axis_index("section"), lax.axis_index("expert"), lax.axis_index("tensor")
    peer = 1 - core
    width = x_ref.shape[1]
    chunks = width // LANES
    half = chunks // 2
    slots = n_expert * cap
    members = n_expert // 2
    quarter = n_expert // 4
    rows = n_tensor * members * cap
    full_rows = lhs.shape[1]
    ff = w1.shape[1]

    def member(g, m):
        return (m // quarter) * (2 * quarter) + g * quarter + lax.rem(m, quarter)

    load1 = pltpu.make_async_copy(w1_hbm, w1, w_sem.at[0])
    load2 = pltpu.make_async_copy(w2_hbm, w2, w_sem.at[1])
    load1.start()
    load2.start()

    barrier = pltpu.get_barrier_semaphore()

    def greet(i, carry):
        pl.semaphore_signal(
            barrier, inc=1, device_id=(peer, lax.rem(e + i, n_expert), t), device_id_type=MESH
        )
        return carry

    lax.fori_loop(0, n_expert, greet, 0)
    for d in range(1, n_tensor):
        pl.semaphore_signal(
            barrier, inc=1, device_id=(core, e, lax.rem(t + d, n_tensor)), device_id_type=MESH
        )

    pad_ids[...] = jnp.full(pad_ids.shape, -1, jnp.int32)
    pad_ids[0:2, 0:tok] = ids_ref[...]
    label_rows = max(16, n_expert)
    labels = lax.broadcasted_iota(jnp.int32, (label_rows, LANES), 0)
    hot = [(labels == pad_ids[k:k + 1, :]) for k in range(2)]
    hot_f = [jnp.where(h, 1.0, 0.0).astype(F32) for h in hot]
    earlier = jnp.where(
        lax.broadcasted_iota(jnp.int32, (LANES, LANES), 0)
        < lax.broadcasted_iota(jnp.int32, (LANES, LANES), 1), 1.0, 0.0
    ).astype(BF16)
    before = [jnp.dot(h.astype(BF16), earlier, preferred_element_type=F32) for h in hot_f]
    before[1] = before[1] + jnp.sum(hot_f[0], axis=1, keepdims=True)
    meta_send[...] = pad_ids[...]
    for k in range(2):
        rank = jnp.sum(hot_f[k] * before[k], axis=0, keepdims=True).astype(jnp.int32)
        pick = pad_ids[k:k + 1, :]
        kept = jnp.logical_and(rank < cap, pick >= 0)
        meta_send[2 + k:3 + k, :] = jnp.where(kept, pick * cap + rank, -1)
    aux_send[0:n_expert, :] = router_t[...].astype(F32)
    aux_send[n_expert:n_expert + 8, :] = jnp.broadcast_to(gain_row[...], (8, width))

    pl.semaphore_wait(barrier, n_expert + n_tensor - 1)

    meta_copy = pltpu.make_async_remote_copy(
        meta_send, meta_recv, meta_sem.at[0], meta_sem.at[1], device_id=(peer, e, t), device_id_type=MESH
    )
    meta_copy.start()
    aux_copy = pltpu.make_async_remote_copy(
        aux_send, aux_recv, aux_sem.at[0], aux_sem.at[1], device_id=(peer, e, t), device_id_type=MESH
    )
    meta_copy.wait()
    aux_copy.start()

    slot_rows = back.shape[0] // half
    slot_labels = lax.broadcasted_iota(jnp.int32, (LANES, LANES), 0)
    place = [slot_labels == meta_recv[2 + k:3 + k, :] for k in range(2)]
    place_f = [jnp.where(m, 1.0, 0.0).astype(F32) for m in place]
    spread = (place_f[0] + place_f[1])[0:slot_rows, 0:tok].astype(BF16)
    rows_f = jnp.dot(spread, x_ref[...], preferred_element_type=F32)
    for c in range(chunks):
        gathered[pl.ds(c, slots, stride=chunks), :] = rows_f[0:slots, c * LANES:(c + 1) * LANES]
    disp[...] = gathered[...].reshape(disp.shape).astype(BF16)

    def disp_copy(i):
        target = flip(e, i, n_expert)
        return pltpu.make_async_remote_copy(
            disp.at[target], got.at[0, i], disp_ss.at[i], disp_rs.at[i],
            device_id=(peer, target, t), device_id_type=MESH,
        )

    def fwd_copy(d, i, sending):
        there = (n_tensor - d) if sending else d
        return pltpu.make_async_remote_copy(
            got.at[0, i], got.at[there, i], fwd_ss.at[d, i], fwd_rs.at[there, i],
            device_id=(core, e, lax.rem(t + d, n_tensor)), device_id_type=MESH,
        )

    for g in range(2):
        def send_disp(m, carry, g=g):
            disp_copy(member(g, m)).start()
            return carry

        lax.fori_loop(0, members, send_disp, 0)

    if full_rows > rows:
        for g in range(2):
            flat[g, rows * chunks:full_rows * chunks, :] = jnp.zeros(((full_rows - rows) * chunks, LANES), F32)

    def normalise(g, d, m):
        piece = got[d, member(g, m)].astype(F32).reshape(cap, chunks, LANES)
        total = jnp.sum(jnp.sum(piece * piece, axis=1, keepdims=True), axis=2, keepdims=True)
        scale = lax.rsqrt(total * (1.0 / width) + 1e-05)
        normed = (piece * scale * gain_slab[...][None]).astype(BF16).astype(F32)
        start = pl.multiple_of((d * members + m) * (cap * chunks), cap * chunks)
        flat[g, pl.ds(start, cap * chunks), :] = normed.reshape(cap * chunks, LANES)

    def take(g):
        def one(m, carry):
            disp_copy(member(g, m)).wait_recv()
            for d in range(1, n_tensor):
                fwd_copy(d, member(g, m), True).start()
            normalise(g, 0, m)
            return carry

        lax.fori_loop(0, members, one, 0)

    def take_forwarded(g):
        for d in range(1, n_tensor):
            def one(m, carry, d=d):
                fwd_copy(d, member(g, m), False).wait_recv()
                normalise(g, d, m)
                return carry

            lax.fori_loop(0, members, one, 0)
        for c in range(chunks):
            lhs[g, :, c * LANES:(c + 1) * LANES] = flat[g, pl.ds(c, full_rows, stride=chunks), :].astype(BF16)

    tile = 256

    def first(g):
        def one(n, carry):
            cols = pl.ds(pl.multiple_of(n * tile, tile), tile)
            value = jnp.dot(lhs[g], w1[:, cols], preferred_element_type=F32)
            hid[g, :, cols] = jax.nn.gelu(value).astype(BF16)
            return carry

        lax.fori_loop(0, ff // tile, one, 0)

    def part_copy(h, d, i, sending):
        there = (n_tensor - d) if sending else d
        return pltpu.make_async_remote_copy(
            part_send.at[h, d, i], part_recv.at[h, there, i], part_ss.at[h, d, i], part_rs.at[h, there, i],
            device_id=(core, e, lax.rem(t + d, n_tensor)), device_id_type=MESH,
        )

    def ret_copy(h, i, sending):
        target = flip(e, i, n_expert)
        where = e if sending else target
        return pltpu.make_async_remote_copy(
            ret_send.at[h, i], ret_recv.at[h, where], ret_ss.at[h, i], ret_rs.at[h, where],
            device_id=(peer, target, t), device_id_type=MESH,
        )

    piece_rows = cap * half

    def second(g, h):
        def one(n, carry):
            cols = pl.ds(pl.multiple_of(h * half * LANES + n * tile, tile), tile)
            value = jnp.dot(hid[g], w2[:, cols], preferred_element_type=F32)
            for j in range(tile // LANES):
                partial[g, h, pl.ds(n * (tile // LANES) + j, rows, stride=half), :] = (
                    value[0:rows, j * LANES:(j + 1) * LANES]
                )
            return carry

        lax.fori_loop(0, half * LANES // tile, one, 0)
        for d in range(1, n_tensor):
            def send_part(k, carry, d=d):
                m = members - 1 - k
                i = member(g, m)
                start = pl.multiple_of((d * members + m) * piece_rows, piece_rows)
                part_send[h, d, i] = partial[g, h, pl.ds(start, piece_rows), :].astype(BF16)
                part_copy(h, d, i, True).start()
                return carry

            lax.fori_loop(0, members, send_part, 0)

    def reduce(g, h):
        def one(k, carry):
            m = members - 1 - k
            i = member(g, m)
            start = pl.multiple_of(m * piece_rows, piece_rows)
            total = partial[g, h, pl.ds(start, piece_rows), :].astype(BF16).astype(F32)
            for d in range(1, n_tensor):
                part_copy(h, d, i, False).wait_recv()
                total = total + part_recv[h, d, i].astype(F32)
            ret_send[h, i] = total.astype(BF16)
            ret_copy(h, i, True).start()
            return carry

        lax.fori_loop(0, members, one, 0)

    take(0)
    take_forwarded(0)
    load1.wait()
    first(0)
    take(1)
    load2.wait()
    second(0, 0)
    second(0, 1)
    take_forwarded(1)
    reduce(0, 0)
    first(1)
    reduce(0, 1)
    second(1, 0)
    second(1, 1)
    reduce(1, 0)
    reduce(1, 1)

    aux_copy.wait()
    x_f = x_ref[...].astype(F32)
    mean_sq = jnp.mean(x_f * x_f, axis=-1, keepdims=True)
    normed = (x_f * lax.rsqrt(mean_sq + 1e-05) * aux_recv[n_expert:n_expert + 1, :]).astype(BF16)
    logit_pad[...] = jnp.zeros(logit_pad.shape, F32)
    logit_pad[0:n_expert, 0:tok] = lax.dot_general(
        aux_recv[0:n_expert, :].astype(BF16), normed, (((1,), (1,)), ((), ())), preferred_element_type=F32
    )
    squashed = []
    for k in range(2):
        hit = labels == meta_recv[k:k + 1, :]
        squashed.append(
            jax.nn.sigmoid(jnp.sum(jnp.where(hit, logit_pad[...], 0.0), axis=0, keepdims=True))
        )
    both = squashed[0] + squashed[1]
    weights = place_f[0] * (squashed[0] / both) + place_f[1] * (squashed[1] / both)
    combine = jnp.transpose(weights)[0:tok, 0:slot_rows]
    high = combine.astype(BF16)
    rest = combine - high.astype(F32)
    mid = rest.astype(BF16)
    low = (rest - mid.astype(F32)).astype(BF16)
    if slot_rows > slots:
        back[slots * half:slot_rows * half, :] = jnp.zeros(((slot_rows - slots) * half, LANES), F32)

    for h in range(2):
        def arrive(i, carry, h=h):
            ret_copy(h, i, False).wait_recv()
            return carry

        lax.fori_loop(0, n_expert, arrive, 0)
        back[0:slots * half, :] = ret_recv[h].reshape(slots * half, LANES).astype(F32)
        table = jnp.concatenate(
            [back[pl.ds(c, slot_rows, stride=half), :].astype(BF16) for c in range(half)], axis=1
        )
        cols = slice(h * half * LANES, (h + 1) * half * LANES)
        added = jnp.dot(high, table, preferred_element_type=F32)
        added = added + jnp.dot(mid, table, preferred_element_type=F32)
        added = added + jnp.dot(low, table, preferred_element_type=F32)
        out_ref[:, cols] = (x_ref[:, cols].astype(F32) + added).astype(BF16)

    def drain(i, carry):
        disp_copy(i).wait_send()
        for d in range(1, n_tensor):
            fwd_copy(d, i, True).wait_send()
        for h in range(2):
            ret_copy(h, i, True).wait_send()
            for d in range(1, n_tensor):
                part_copy(h, d, i, True).wait_send()
        return carry

    lax.fori_loop(0, n_expert, drain, 0)


def on_device(sent, norm_gain, router, w_in, w_out, expert_ids):
    tok, width = sent.shape[1], sent.shape[2]
    n_expert, n_tensor = lax.axis_size("expert"), lax.axis_size("tensor")
    top = expert_ids.shape[2]
    ff = w_in.shape[3]
    cap = max(2, (5 * top * tok + 4 * n_expert - 1) // (4 * n_expert))
    slots = n_expert * cap
    slot_rows = -(-slots // 16) * 16
    rows = n_tensor * slots // 2
    full_rows = -(-rows // 16) * 16
    chunks = width // LANES
    half = chunks // 2
    vmem = pl.BlockSpec(memory_space=pltpu.VMEM)
    hbm = pl.BlockSpec(memory_space=pl.ANY)
    dma = pltpu.SemaphoreType.DMA
    result = pl.pallas_call(
        functools.partial(kernel, n_expert, n_tensor, cap, tok),
        out_shape=jax.ShapeDtypeStruct((tok, width), BF16),
        in_specs=[vmem, vmem, vmem, vmem, vmem, hbm, hbm],
        out_specs=vmem,
        scratch_shapes=[
            pltpu.VMEM((width, ff), BF16),
            pltpu.VMEM((ff, width), BF16),
            pltpu.VMEM((8, LANES), jnp.int32),
            pltpu.VMEM((8, LANES), jnp.int32),
            pltpu.VMEM((8, LANES), jnp.int32),
            pltpu.VMEM((n_expert + 8, width), F32),
            pltpu.VMEM((n_expert + 8, width), F32),
            pltpu.VMEM((max(16, n_expert), LANES), F32),
            pltpu.VMEM((slots * chunks, LANES), F32),
            pltpu.VMEM((n_expert, cap * chunks, LANES), BF16),
            pltpu.VMEM((n_tensor, n_expert, cap * chunks, LANES), BF16),
            pltpu.VMEM((2, full_rows * chunks, LANES), F32),
            pltpu.VMEM((2, full_rows, width), BF16),
            pltpu.VMEM((2, full_rows, ff), BF16),
            pltpu.VMEM((2, 2, rows * half, LANES), F32),
            pltpu.VMEM((2, n_tensor, n_expert, cap * half, LANES), BF16),
            pltpu.VMEM((2, n_tensor, n_expert, cap * half, LANES), BF16),
            pltpu.VMEM((2, n_expert, cap * half, LANES), BF16),
            pltpu.VMEM((2, n_expert, cap * half, LANES), BF16),
            pltpu.VMEM((slot_rows * half, LANES), F32),
            dma((2,)),
            dma((2,)),
            dma((2,)),
            dma((n_expert,)),
            dma((n_expert,)),
            dma((n_tensor, n_expert)),
            dma((n_tensor, n_expert)),
            dma((2, n_tensor, n_expert)),
            dma((2, n_tensor, n_expert)),
            dma((2, n_expert)),
            dma((2, n_expert)),
        ],
        compiler_params=pltpu.CompilerParams(
            collective_id=0, has_side_effects=True, vmem_limit_bytes=56 * 2**20
        ),
        name="expert_layer",
    )(
        sent[0],
        norm_gain.reshape(chunks, LANES),
        norm_gain,
        jnp.transpose(router[0]),
        jnp.transpose(expert_ids[0]),
        w_in[0, 0],
        w_out[0, 0],
    )
    return result[None]


def solution(mesh):
    return jax.shard_map(
        on_device,
        mesh=mesh,
        in_specs=(
            P("section", ("expert", "tensor"), None),
            P("section", None),
            P("section", None, None),
            P("section", "expert", None, "tensor"),
            P("section", "expert", "tensor", None),
            P("section", ("expert", "tensor"), None),
        ),
        out_specs=P("section", ("expert", "tensor"), None),
        check_vma=False,
    )
```
